256 devices in a mesh: grp: 8 (over z), sfc: 32 (over y, x, core).
Axes of the slice: x: 4, y: 4, z: 8, core: 2. Of those that a mesh axis runs over, the one named last changes fastest.
Arguments:
- old_coef: bfloat16 [64, 64, 32768], P(None, None, ('grp', 'sfc')), may hold values from 0.5 to 8
- refine_flags: int32 [32768], P(('grp', 'sfc')), may hold values from 0 to 1, as said below
- counts: int32 [256], P(('grp', 'sfc')), may hold values from 1 to 128, as said below
- right_side: float32 [64, 64, 32768], P(None, None, ('grp', 'sfc')), may hold values from -6 to 6
- nbr_first: int32 [4, 32768], P(None, ('grp', 'sfc')), may hold values from 0 to 32767, as said below
- nbr_second: int32 [4, 32768], P(None, ('grp', 'sfc')), may hold values from 0 to 32767, as said below
- face_kind: int32 [4, 32768], P(None, ('grp', 'sfc')), may hold values from 0 to 4
Outputs:
- solution: float32 [64, 64, 32768], P(None, None, ('grp', 'sfc'))
- residual: float32 [64, 64, 32768], P(None, None, ('grp', 'sfc'))
The draws below stay inside these ranges and needn't reach their ends.
Inputs may be any that keep to these rules, and one draw needn't show every extreme that they name: `refine_flags`: 0 or 1; 0 in the slots of a device at or past its count. The number of new leaves, count + 3 * (flags) of a device, summed over devices 0 .. e (the flattened index over grp then sfc) is (e + 1) * 128 + drift_e with 0 <= drift_e <= 63, drift 0 at the last device and 63 at some device. `counts`: old leaves fill the first slots of a device. `nbr_first`: global new leaf index; the device owning it sits at the same grp and sfc index as the leaf's owner or differs by one in exactly one of the two. Equal to the leaf itself for face_kind 0. `nbr_second`: as nbr_first, and equal to it unless face_kind is 4; then on the same device as nbr_first.
All inputs are finite; a program needn't handle non-finite values.
Results may differ from the reference program's by a relative error of at most 0.0003.
Values may be sent and summed in bfloat16 or wider, within the bound.
No kernel may reach another device: no remote copies, remote signals or barrier semaphores. Data moves between devices by JAX's collectives and lax.ppermute only.
A program may use at most 128 MiB of HBM per device.

```python
import math
import jax
import jax.numpy as jnp

B = 64
LEAF_DEV = 128
LEAVES = 32768
N_GRP = 8
N_SFC = 32


def leaf_plan(key):
    devices_all = N_GRP * N_SFC
    per_device = LEAF_DEV
    reach = per_device // 2
    keys = jax.random.split(key, 4)
    device_ids = jnp.arange(devices_all, dtype=jnp.int32)
    drift = jax.random.randint(keys[0], (devices_all,), 0, reach, dtype=jnp.int32)
    peak_dev = jax.random.randint(keys[1], (), 0, devices_all - 1, dtype=jnp.int32)
    drift = jnp.where(device_ids == peak_dev, reach - 1, drift)
    drift = jnp.where(device_ids == devices_all - 1, 0, drift)
    earlier = jnp.concatenate([jnp.zeros((1,), jnp.int32), drift[:-1]])
    produced = per_device + drift - earlier
    least = jnp.maximum(0, (produced - per_device + 2) // 3)
    flagged = jax.random.randint(keys[2], (devices_all,), least, produced // 4 + 1, dtype=jnp.int32)
    counts = (produced - 3 * flagged).astype(jnp.int32)
    orders = jax.vmap(lambda sub_key: jax.random.permutation(sub_key, per_device))(jax.random.split(keys[3], devices_all))
    slot_index = jnp.arange(per_device, dtype=jnp.int32)[None, :]
    occupied = slot_index < counts[:, None]
    smaller = (orders[:, None, :] < orders[:, :, None]) & occupied[:, None, :]
    ranking = jnp.sum(smaller.astype(jnp.int32), axis=2)
    flags_all = (occupied & (ranking < flagged[:, None])).astype(jnp.int32)
    return (counts, flags_all.reshape(-1))


def neighbour_plan(key):
    per_device = LEAF_DEV
    leaf_total = per_device * N_GRP * N_SFC
    keys = jax.random.split(key, 4)
    leaf_ids = jnp.broadcast_to(jnp.arange(leaf_total, dtype=jnp.int32)[None, :], (4, leaf_total))
    owner_dev = leaf_ids // per_device
    grp_pos = owner_dev // N_SFC
    sfc_pos = owner_dev % N_SFC
    kind_table = jnp.array([0, 1, 1, 1, 1, 1, 1, 1, 1, 2, 2, 3, 3, 4, 4, 4], jnp.int32)
    kinds = kind_table[jax.random.randint(keys[0], (4, leaf_total), 0, 16, dtype=jnp.int32)]
    direction = jax.random.randint(keys[1], (4, leaf_total), 0, 8, dtype=jnp.int32)
    grp_steps = jnp.array([0, 0, 0, 0, -1, 1, 0, 0], jnp.int32)[direction]
    sfc_steps = jnp.array([0, 0, 0, 0, 0, 0, -1, 1], jnp.int32)[direction]
    grp_to = grp_pos + grp_steps
    sfc_to = sfc_pos + sfc_steps
    outside = (grp_to < 0) | (grp_to >= N_GRP) | (sfc_to < 0) | (sfc_to >= N_SFC)
    kinds = jnp.where(outside, 0, kinds)
    home = (jnp.clip(grp_to, 0, N_GRP - 1) * N_SFC + jnp.clip(sfc_to, 0, N_SFC - 1)) * per_device
    leading = home + jax.random.randint(keys[2], (4, leaf_total), 0, per_device, dtype=jnp.int32)
    trailing = home + jax.random.randint(keys[3], (4, leaf_total), 0, per_device, dtype=jnp.int32)
    leading = jnp.where(kinds == 0, leaf_ids, leading)
    trailing = jnp.where(kinds == 4, trailing, leading)
    return (leading.astype(jnp.int32), trailing.astype(jnp.int32), kinds.astype(jnp.int32))


def draw_refine_flags(key, part):
    planned = leaf_plan(key)
    return planned[1]


def draw_counts(key, part):
    planned = leaf_plan(key)
    return planned[0]


def draw_nbr_first(key, part):
    planned = neighbour_plan(key)
    return planned[0]


def draw_nbr_second(key, part):
    planned = neighbour_plan(key)
    return planned[1]


def draw_face_kind(key, part):
    planned = neighbour_plan(key)
    return planned[2]


def levels(rng, shape, cuts, smallest, largest):
    factor_of, own = 1.0, jax.random.fold_in(rng, 6)
    for position, shards_of in cuts:
        heights = jnp.exp(jax.random.uniform(jax.random.fold_in(own, position), (shards_of,), jnp.float32, smallest / len(cuts), largest / len(cuts)))
        factor_of = factor_of * jnp.repeat(heights, shape[position] // shards_of).reshape([-1 if axis == position else 1 for axis in range(len(shape))])
    return factor_of


def scatter_about(stream_key, dims, spread, most, cuts=(), kind=jnp.bfloat16):
    values = spread * jax.random.normal(stream_key, dims, jnp.float32)
    if cuts:
        values = values * levels(stream_key, dims, cuts, -0.22, 0.18)
    return jnp.clip(values, -most, most).astype(kind)


def setup_inputs(seed: int = 0) -> dict:
    arg_keys = jax.random.split(jax.random.key(seed), 8)
    old_coef = jnp.clip(jnp.exp(math.log(8.0) - 2.7725887 * jax.random.uniform(arg_keys[0], (B, B, LEAVES), jnp.float32) ** levels(arg_keys[0], (B, B, LEAVES), ((2, 256),), -0.2, 0.2)), 0.5, 8.0).astype(jnp.bfloat16)
    refine_flags = draw_refine_flags(jax.random.fold_in(arg_keys[7], 71), 0)
    counts = draw_counts(jax.random.fold_in(arg_keys[7], 71), 0)
    right_side = scatter_about(arg_keys[3], (B, B, LEAVES), 1.0, 6.0, ((2, 256),), jnp.float32)
    nbr_first = draw_nbr_first(jax.random.fold_in(arg_keys[7], 71), 0)
    nbr_second = draw_nbr_second(jax.random.fold_in(arg_keys[7], 71), 0)
    face_kind = draw_face_kind(jax.random.fold_in(arg_keys[7], 71), 0)
    return {"old_coef": old_coef, "refine_flags": refine_flags, "counts": counts, "right_side": right_side, "nbr_first": nbr_first, "nbr_second": nbr_second, "face_kind": face_kind}


LOWER_BOUND = 0.3
UPPER_BOUND = 1.9


def refine(coef_blocks, parent, child_index, quadrant):
    extent = coef_blocks.shape[0]
    halfway = extent // 2
    picked = jnp.take(coef_blocks, parent, axis=2)
    leaf_count = picked.shape[2]
    quarters = picked.reshape(2, halfway, 2, halfway, leaf_count)
    first_bit = (child_index % 2) == 1
    second_bit = (child_index // 2) == 1
    rows_picked = jnp.where(first_bit[None, None, None, :], quarters[1], quarters[0])
    chosen = jnp.where(second_bit[None, None, :], rows_picked[:, 1], rows_picked[:, 0])
    doubled = jnp.broadcast_to(chosen[:, None, :, None, :], (halfway, 2, halfway, 2, leaf_count)).reshape(extent, extent, leaf_count)
    return jnp.where(quadrant[None, None, :], doubled, picked)


def boundary(iterate):
    return jnp.stack([iterate[0], iterate[-1], iterate[:, 0], iterate[:, -1]], axis=1)


def facing_index():
    face_ids = jnp.arange(4, dtype=jnp.int32)[:, None]
    return (face_ids + 1 - 2 * (face_ids % 2)).astype(jnp.int32)


def hang(leading, second, face_kind):
    halfway = leading.shape[0] // 2
    lower_half = jnp.repeat(leading[:halfway], 2, axis=0)
    upper_half = jnp.repeat(leading[halfway:], 2, axis=0)
    coarse = jnp.concatenate([leading[0::2] + leading[1::2], second[0::2] + second[1::2]], axis=0) * 0.5
    return jnp.where(face_kind == 1, leading, jnp.where(face_kind == 2, lower_half, jnp.where(face_kind == 3, upper_half, jnp.where(face_kind == 4, coarse, jnp.zeros_like(leading)))))


def apply_operator(iterate, diagonal, ghost):
    upward = jnp.concatenate([ghost[:, 0][None], iterate[:-1]], axis=0)
    downward = jnp.concatenate([iterate[1:], ghost[:, 1][None]], axis=0)
    leftward = jnp.concatenate([ghost[:, 2][:, None], iterate[:, :-1]], axis=1)
    rightward = jnp.concatenate([iterate[:, 1:], ghost[:, 3][:, None]], axis=1)
    return diagonal * iterate - (upward + downward + leftward + rightward)


def chebyshev(right_side, diagonal, ghost_of):
    middle = (UPPER_BOUND + LOWER_BOUND) / 2.0
    radius = (UPPER_BOUND - LOWER_BOUND) / 2.0
    spread_ratio = middle / radius
    factor = 1.0 / spread_ratio
    update = right_side / diagonal / middle
    solution = jnp.zeros_like(right_side)
    residual = right_side
    for iteration in range(3):
        solution = solution + update
        residual = right_side - apply_operator(solution, diagonal, ghost_of(boundary(solution)))
        if iteration < 2:
            factor_next = 1.0 / (2.0 * spread_ratio - factor)
            update = (factor_next * factor) * update + (2.0 * factor_next / radius) * (residual / diagonal)
            factor = factor_next
    return solution, residual


def reference(old_coef, refine_flags, counts, right_side, nbr_first, nbr_second, face_kind):
    per_device = refine_flags.shape[0] // counts.shape[0]
    slot_index = (jnp.arange(refine_flags.shape[0], dtype=jnp.int32) % per_device).astype(jnp.int32)
    occupied = slot_index < jnp.repeat(counts, per_device)
    weight = jnp.where(occupied, 1 + 3 * refine_flags, 0).astype(jnp.int32)
    inclusive = jnp.cumsum(weight).astype(jnp.int32)
    starts = (inclusive - weight).astype(jnp.int32)
    targets = jnp.arange(right_side.shape[2], dtype=jnp.int32)
    parent = jnp.searchsorted(inclusive, targets, side="right").astype(jnp.int32)
    child_index = (targets - jnp.take(starts, parent)).astype(jnp.int32)
    quadrant = jnp.take(weight, parent) == 4
    coefficient = refine(old_coef, parent, child_index, quadrant)
    diagonal = 4.0 + coefficient.astype(jnp.float32)
    leaf_total = right_side.shape[2]
    facing = facing_index()
    index_first = (facing * leaf_total + nbr_first).astype(jnp.int32).reshape(-1)
    index_second = (facing * leaf_total + nbr_second).astype(jnp.int32).reshape(-1)

    def ghost_of(face_values):
        flattened = face_values.reshape(face_values.shape[0], -1)
        leading = jnp.take(flattened, index_first, axis=1).reshape(face_values.shape)
        second = jnp.take(flattened, index_second, axis=1).reshape(face_values.shape)
        return hang(leading, second, face_kind)

    return chebyshev(right_side, diagonal, ghost_of)
```

```python
import functools

import jax
import jax.numpy as jnp
from jax import lax
from jax.experimental import pallas as pl
from jax.experimental.pallas import tpu as pltpu
from jax.sharding import PartitionSpec as P

LOWER_BOUND = 0.3
UPPER_BOUND = 1.9
B = 64
ROWS = B * B
LANES = 128
AXES = ("grp", "sfc")

THETA = (UPPER_BOUND + LOWER_BOUND) / 2.0
DELTA = (UPPER_BOUND - LOWER_BOUND) / 2.0
SIGMA = THETA / DELTA
RHO_0 = 1.0 / SIGMA
RHO_1 = 1.0 / (2.0 * SIGMA - RHO_0)
RHO_2 = 1.0 / (2.0 * SIGMA - RHO_1)
C_1, K_1 = RHO_1 * RHO_0, 2.0 * RHO_1 / DELTA
C_2, K_2 = RHO_2 * RHO_1, 2.0 * RHO_2 / DELTA

F32 = jnp.float32
VMEM_LIMIT = 40 * 1024 * 1024


def in_vmem(array):
    return pltpu.with_memory_space_constraint(array, pltpu.VMEM)


def call(kernel, outs, scratch, smem, operands, flops):
    specs = [pl.BlockSpec(memory_space=pltpu.SMEM)] * smem
    specs += [pl.BlockSpec(memory_space=pltpu.VMEM)] * (len(operands) - smem)
    return pl.pallas_call(
        kernel,
        out_shape=outs,
        in_specs=specs,
        out_specs=[pl.BlockSpec(memory_space=pltpu.VMEM)] * len(outs),
        scratch_shapes=scratch,
        compiler_params=pltpu.CompilerParams(vmem_limit_bytes=VMEM_LIMIT),
        cost_estimate=pl.CostEstimate(flops=flops, bytes_accessed=4 << 20, transcendentals=0),
    )(*operands[:smem], *[in_vmem(a) for a in operands[smem:]])


def vmem(rows, dtype=F32):
    return pltpu.VMEM((rows, LANES), dtype)


def kept(rows, dtype=F32):
    return pltpu.VMEM((rows, LANES), dtype)


def lane_plan(position, weights_ref):
    rows = lax.broadcasted_iota(jnp.int32, weights_ref.shape, 0)
    before = jnp.where(rows < position, weights_ref[...], 0).astype(F32)
    made = jnp.sum(jnp.sum(before, axis=0, keepdims=True), axis=1, keepdims=True)
    drift = made - (position * LANES).astype(F32)
    own = weights_ref[pl.ds(position, 1), :].astype(F32)
    prev = weights_ref[pl.ds(jnp.maximum(position - 1, 0), 1), :].astype(F32)
    prev = jnp.where(position > 0, prev, 0.0)
    window = 2 * LANES
    spread = jnp.broadcast_to(jnp.concatenate([prev, own], axis=1), (LANES, window)).astype(jnp.bfloat16)
    slot = lax.broadcasted_iota(jnp.int32, (window, window), 0)
    other = lax.broadcasted_iota(jnp.int32, (window, window), 1)
    lower = jnp.where(other <= slot, 1.0, 0.0).astype(jnp.bfloat16)
    inclusive = lax.dot_general(
        lower, spread, (((1,), (1,)), ((), ())), preferred_element_type=F32
    )
    before_own = inclusive[LANES - 1 : LANES]
    inclusive = inclusive - before_own
    target = lax.broadcasted_iota(jnp.int32, (1, LANES), 1).astype(F32) - drift
    passed = inclusive <= target
    parent = jnp.sum(jnp.where(passed, 1.0, 0.0), axis=0, keepdims=True)
    start = jnp.max(jnp.where(passed, inclusive, -before_own), axis=0, keepdims=True)
    stop = jnp.min(jnp.where(passed, 1e6, inclusive), axis=0, keepdims=True)
    child = target - start
    slot_f = lax.broadcasted_iota(jnp.int32, (window, LANES), 0).astype(F32)
    one_hot = jnp.where(slot_f == parent, 1.0, 0.0).astype(jnp.bfloat16)
    refined = (stop - start) > 2.0
    first_bit = (child == 1.0) | (child == 3.0)
    second_bit = child >= 2.0
    return one_hot, refined, first_bit, second_bit


def take_faces(field_ref, faces_ref):
    faces_ref[0:B] = field_ref[0:B]
    faces_ref[B : 2 * B] = field_ref[ROWS - B : ROWS]
    faces_ref[2 * B : 3 * B] = field_ref[pl.ds(0, B, stride=B)]
    faces_ref[3 * B : 4 * B] = field_ref[pl.ds(B - 1, B, stride=B)]


def build_kernel(position_ref, weights_ref, prev_ref, own_ref, right_ref, s_ref, inv_ref, diag_ref, faces_ref, pick_ref, dup_ref):
    one_hot, refined, first_bit, second_bit = lane_plan(position_ref[0], weights_ref)
    chunk = 512

    def pick(step, carry):
        at = pl.ds(pl.multiple_of(step * chunk, chunk), chunk)
        both = jnp.concatenate([prev_ref[at], own_ref[at]], axis=1)
        pick_ref[at] = jnp.dot(both, one_hot, preferred_element_type=F32)
        return carry

    lax.fori_loop(0, ROWS // chunk, pick, 0, unroll=2)
    half = B // 2

    def leaf(row, carry):
        low = pick_ref[pl.ds(pl.multiple_of(row * B, B), B)]
        high = pick_ref[pl.ds(pl.multiple_of((row + half) * B, B), B)]
        chosen = jnp.where(first_bit, high, low)
        chosen = jnp.where(second_bit, chosen[half:], chosen[:half])
        slot = pl.multiple_of((row % 2) * B, B)
        dup_ref[pl.ds(slot, half, stride=2)] = chosen
        dup_ref[pl.ds(slot + 1, half, stride=2)] = chosen
        doubled = dup_ref[pl.ds(slot, B)]
        for k in range(2):
            at = pl.ds(pl.multiple_of((2 * row + k) * B, B), B)
            diag = 4.0 + jnp.where(refined, doubled, pick_ref[at])
            inv = 1.0 / diag
            diag_ref[at] = diag
            inv_ref[at] = inv
            s_ref[at] = right_ref[at] * inv * (1.0 / THETA)
        return carry

    lax.fori_loop(0, half, leaf, 0, unroll=2)
    take_faces(s_ref, faces_ref)


def fill_ghosts(position_ref, sources, first_ref, second_ref, kind_ref, ghost_ref, pair_ref):
    position = position_ref[0]
    half = B // 2
    for face in range(4):
        facing = face ^ 1
        kind = kind_ref[face : face + 1]
        values = []
        for index_ref in (first_ref, second_ref):
            index = index_ref[face : face + 1]
            offset = lax.shift_right_logical(index, 7) - position
            lane = jnp.broadcast_to(index & (LANES - 1), (B, LANES))
            value = jnp.zeros((B, LANES), F32)
            for faces_ref, away in sources:
                taken = jnp.take_along_axis(
                    faces_ref[facing * B : (facing + 1) * B], lane, axis=1, mode="promise_in_bounds"
                )
                value = jnp.where(offset == away, taken, value)
            values.append(value)
        leading, second = values
        at = face * 4 * B
        pair_ref[at : at + B] = leading
        pair_ref[at + B : at + 2 * B] = second
        mean_low = (pair_ref[pl.ds(at, half, stride=2)] + pair_ref[pl.ds(at + 1, half, stride=2)]) * 0.5
        mean_high = (
            pair_ref[pl.ds(at + B, half, stride=2)] + pair_ref[pl.ds(at + B + 1, half, stride=2)]
        ) * 0.5
        for part in range(2):
            for odd in range(2):
                pair_ref[pl.ds(at + (2 + part) * B + odd, half, stride=2)] = leading[
                    part * half : (part + 1) * half
                ]
        ghost = jnp.where(kind == 4, jnp.concatenate([mean_low, mean_high], axis=0), 0.0)
        ghost = jnp.where(kind == 1, leading, ghost)
        ghost = jnp.where(kind == 2, pair_ref[at + 2 * B : at + 3 * B], ghost)
        ghost = jnp.where(kind == 3, pair_ref[at + 3 * B : at + 4 * B], ghost)
        ghost_ref[face * B : (face + 1) * B] = ghost


FACE_SLICES = (pl.ds(0, B), pl.ds(ROWS - B, B), pl.ds(0, B, stride=B), pl.ds(B - 1, B, stride=B))


def sweep(field_ref, finish):
    edge = lax.broadcasted_iota(jnp.int32, (B, LANES), 0)
    is_first, is_last = edge == 0, edge == B - 1

    def plane(index, position):
        at = pl.ds(pl.multiple_of(index * B, B), B)
        centre = field_ref[at]
        if position == 0:
            total = field_ref[pl.ds((index + 1) * B, B)]
        elif position == 2:
            total = field_ref[pl.ds((index - 1) * B, B)]
        else:
            total = field_ref[pl.ds(pl.multiple_of((index - 1) * B, B), B)]
            total = total + field_ref[pl.ds(pl.multiple_of((index + 1) * B, B), B)]
        if position == 0:
            left = pltpu.roll(centre, 1, 0)
        else:
            left = field_ref[pl.ds(index * B - 1, B)]
        if position == 2:
            right = pltpu.roll(centre, B - 1, 0)
        else:
            right = field_ref[pl.ds(index * B + 1, B)]
        total = total + jnp.where(is_first, 0.0, left) + jnp.where(is_last, 0.0, right)
        finish(at, centre, total)

    plane(0, 0)

    def step(index, carry):
        plane(index, 1)
        return carry

    lax.fori_loop(1, B - 1, step, 0, unroll=2)
    plane(B - 1, 2)


def step_kernel(scale_v, scale_u, scale_n, smem_ref, own_ref, *refs):
    received, (first_ref, second_ref, kind_ref, v_ref, u_ref, inv_ref) = refs[:4], refs[4:10]
    out_ref, faces_ref, ghost_ref, pair_ref = refs[10:]
    sources = [(own_ref, 0)] + [(r, smem_ref[1 + i]) for i, r in enumerate(received)]
    fill_ghosts(smem_ref, sources, first_ref, second_ref, kind_ref, ghost_ref, pair_ref)

    def finish(at, centre, total):
        out = scale_v * centre + scale_n * (inv_ref[at] * total)
        if scale_u is not None:
            out = out + scale_u * u_ref[at]
        out_ref[at] = out

    sweep(v_ref, finish)
    for face, at in enumerate(FACE_SLICES):
        out_ref[at] = out_ref[at] + scale_n * (inv_ref[at] * ghost_ref[face * B : (face + 1) * B])
    take_faces(out_ref, faces_ref)


def residual_kernel(smem_ref, own_ref, *refs):
    received, (first_ref, second_ref, kind_ref, v_ref, u_ref, diag_ref) = refs[:4], refs[4:10]
    out_ref, ghost_ref, pair_ref = refs[10:]
    sources = [(own_ref, 0)] + [(r, smem_ref[1 + i]) for i, r in enumerate(received)]
    fill_ghosts(smem_ref, sources, first_ref, second_ref, kind_ref, ghost_ref, pair_ref)

    def finish(at, centre, total):
        out_ref[at] = diag_ref[at] * (THETA * u_ref[at] - centre) + total

    sweep(v_ref, finish)
    for face, at in enumerate(FACE_SLICES):
        out_ref[at] = out_ref[at] + ghost_ref[face * B : (face + 1) * B]


def swap(value, axis, parity):
    count = lax.axis_size(axis)
    pairs = []
    for low in range(parity, count - 1, 2):
        pairs += [(low, low + 1), (low + 1, low)]
    return lax.ppermute(value, axis, pairs)


def exchange(faces):
    return [swap(faces, "sfc", 1), swap(faces, "grp", 1), swap(faces, "grp", 0), swap(faces, "sfc", 0)]


def body(old_coef, refine_flags, counts, right_side, nbr_first, nbr_second, face_kind):
    grp, sfc = lax.axis_index("grp"), lax.axis_index("sfc")
    n_sfc = lax.axis_size("sfc")
    devices = lax.axis_size(AXES)
    position = grp * n_sfc + sfc
    prev_coef = lax.ppermute(old_coef, AXES, [(i, i + 1) for i in range(devices - 1)])
    slots = jnp.arange(LANES, dtype=jnp.int32)
    weight = jnp.where(slots < counts[0], 1 + 3 * refine_flags, 0)
    weights = lax.all_to_all(
        jnp.broadcast_to(weight[None], (devices, LANES)), AXES, 0, 0, tiled=True
    )
    to_odd_sfc, to_odd_grp = 2 * (sfc % 2) - 1, n_sfc * (2 * (grp % 2) - 1)
    scalars = jnp.stack([position, to_odd_sfc, to_odd_grp, -to_odd_grp, -to_odd_sfc]).astype(jnp.int32)

    s1, inv, diag, faces = call(
        build_kernel,
        [kept(ROWS), kept(ROWS), kept(ROWS), kept(4 * B)],
        [vmem(ROWS), vmem(2 * B)],
        1,
        [scalars, weights, prev_coef.reshape(ROWS, LANES), old_coef.reshape(ROWS, LANES), right_side.reshape(ROWS, LANES)],
        300_000_000,
    )
    plan = [nbr_first, nbr_second, face_kind]
    scratch = [vmem(4 * B), vmem(16 * B)]
    s2, faces_2 = call(
        functools.partial(step_kernel, 1.0 + C_1 + K_1 * (THETA - 1.0), None, K_1),
        [kept(ROWS), kept(4 * B)],
        scratch,
        1,
        [scalars, faces, *exchange(faces), *plan, s1, s1, inv],
        10_000_000,
    )
    s3, faces_3 = call(
        functools.partial(step_kernel, 1.0 + C_2 - K_2, K_2 * THETA - C_2, K_2),
        [kept(ROWS), kept(4 * B)],
        scratch,
        1,
        [scalars, faces_2, *exchange(faces_2), *plan, s2, s1, inv],
        10_000_000,
    )
    (residual,) = call(
        residual_kernel,
        [jax.ShapeDtypeStruct((ROWS, LANES), F32)],
        scratch,
        1,
        [scalars, faces_3, *exchange(faces_3), *plan, s3, s1, diag],
        10_000_000,
    )
    return s3.reshape(B, B, LANES), residual.reshape(B, B, LANES)


def solution(mesh):
    leaves, lines = P(None, None, AXES), P(None, AXES)
    return jax.shard_map(
        body,
        mesh=mesh,
        in_specs=(leaves, P(AXES), P(AXES), leaves, lines, lines, lines),
        out_specs=(leaves, leaves),
        check_vma=False,
    )
```

```python
import functools

import jax
import jax.numpy as jnp
from jax import lax
from jax.experimental import pallas as pl
from jax.experimental.pallas import tpu as pltpu
from jax.sharding import PartitionSpec as P

LOWER_BOUND = 0.3
UPPER_BOUND = 1.9
B = 64
ROWS = B * B
LANES = 128
AXES = ("grp", "sfc")

THETA = (UPPER_BOUND + LOWER_BOUND) / 2.0
DELTA = (UPPER_BOUND - LOWER_BOUND) / 2.0
SIGMA = THETA / DELTA
RHO_0 = 1.0 / SIGMA
RHO_1 = 1.0 / (2.0 * SIGMA - RHO_0)
RHO_2 = 1.0 / (2.0 * SIGMA - RHO_1)
C_1, K_1 = RHO_1 * RHO_0, 2.0 * RHO_1 / DELTA
C_2, K_2 = RHO_2 * RHO_1, 2.0 * RHO_2 / DELTA

F32 = jnp.float32
VMEM_LIMIT = 32 * 1024 * 1024


def placed(array, space):
    return array if space in (SMEM, ANY, FREE) else pltpu.with_memory_space_constraint(array, SPACES[space])


def vmem(rows, dtype=F32):
    return pltpu.VMEM((rows, LANES), dtype)


def kept(rows, dtype=F32, lanes=LANES):
    return pltpu.VMEM((rows, lanes), dtype)


def in_hbm(shape):
    return pltpu.HBM(shape, F32)


SMEM, VMEM, HBM, ANY, FREE = "smem", "vmem", "hbm", "any", "free"
SPACES = {FREE: pltpu.VMEM, SMEM: pltpu.SMEM, VMEM: pltpu.VMEM, HBM: pltpu.HBM, ANY: pl.ANY}


def call(kernel, operands, outs, scratch=(), aliases=None, flops=1_000_000):
    specs = [pl.BlockSpec(memory_space=SPACES[space]) for _, space in operands]
    return pl.pallas_call(
        kernel,
        out_shape=[shape for shape, _ in outs],
        in_specs=specs,
        out_specs=[pl.BlockSpec(memory_space=SPACES[space]) for _, space in outs],
        scratch_shapes=list(scratch),
        input_output_aliases=aliases or {},
        compiler_params=pltpu.CompilerParams(vmem_limit_bytes=VMEM_LIMIT),
        cost_estimate=pl.CostEstimate(flops=flops, bytes_accessed=flops, transcendentals=0),
    )(*[placed(array, space) for array, space in operands])


FACE_SLICES = (pl.ds(0, B), pl.ds(ROWS - B, B), pl.ds(0, B, stride=B), pl.ds(B - 1, B, stride=B))
LINES = (0, B // 2 - 1, B // 2, B - 1)


def face(index):
    return pl.ds(index * B, B)


def weights_kernel(count_ref, flags_ref, out_ref):
    slot = lax.broadcasted_iota(jnp.int32, (1, LANES), 1)
    weight = jnp.where(slot < count_ref[0], 1 + 3 * flags_ref[...], 0)
    out_ref[...] = jnp.broadcast_to(weight, out_ref.shape)


def stage_kernel(prev_in, own_in, right_in, staged_ref, prev_ref, own_ref, wide_ref, edge_ref, faces_ref, sems):
    blocks = [
        pltpu.make_async_copy(of, to, sems.at[k])
        for k, (of, to) in enumerate(((prev_in, prev_ref), (own_in, own_ref)))
    ]
    reads = []
    for k in range(2):
        reads.append(pltpu.make_async_copy(right_in.at[k * (B - 1)], faces_ref.at[face(k)], sems.at[2 + k]))
        of = right_in.at[:, pl.ds(k * (B - 8), 8)]
        reads.append(pltpu.make_async_copy(of, edge_ref.at[k], sems.at[4 + k]))
    for read in (*blocks, *reads):
        read.start()
    for side, ref in enumerate((prev_ref, own_ref)):
        blocks[side].wait()
        lanes = slice(side * LANES, (side + 1) * LANES)
        wide_ref[...] = ref[...].astype(F32)
        for k, line in enumerate(LINES):
            staged_ref[face(k), lanes] = ref[face(line)]
            staged_ref[face(4 + k), lanes] = wide_ref[pl.ds(line, B, stride=B)].astype(jnp.bfloat16)
    for read in reads:
        read.wait()
    for k in range(2):
        faces_ref[face(2 + k)] = edge_ref[k, :, 7 * k, :]
    left = jnp.concatenate([faces_ref[0 : 2 * B], faces_ref[2 * B : 4 * B]], axis=1)
    for piece in range(3):
        part = left.astype(jnp.bfloat16)
        staged_ref[(8 + 2 * piece) * B : (10 + 2 * piece) * B] = part
        left = left - part.astype(F32)


def lane_plan(position, weights_ref):
    rows = lax.broadcasted_iota(jnp.int32, weights_ref.shape, 0)
    before = jnp.where(rows < position, weights_ref[...], 0).astype(F32)
    made = jnp.sum(jnp.sum(before, axis=0, keepdims=True), axis=1, keepdims=True)
    drift = made - (position * LANES).astype(F32)
    own = weights_ref[pl.ds(position, 1), :].astype(F32)
    prev = weights_ref[pl.ds(jnp.maximum(position - 1, 0), 1), :].astype(F32)
    prev = jnp.where(position > 0, prev, 0.0)
    window = 2 * LANES
    spread = jnp.broadcast_to(jnp.concatenate([prev, own], axis=1), (LANES, window)).astype(jnp.bfloat16)
    slot = lax.broadcasted_iota(jnp.int32, (window, window), 0)
    other = lax.broadcasted_iota(jnp.int32, (window, window), 1)
    lower = jnp.where(other <= slot, 1.0, 0.0).astype(jnp.bfloat16)
    inclusive = lax.dot_general(
        lower, spread, (((1,), (1,)), ((), ())), preferred_element_type=F32
    )
    before_own = inclusive[LANES - 1 : LANES]
    inclusive = inclusive - before_own
    target = lax.broadcasted_iota(jnp.int32, (1, LANES), 1).astype(F32) - drift
    passed = inclusive <= target
    parent = jnp.sum(jnp.where(passed, 1.0, 0.0), axis=0, keepdims=True)
    start = jnp.max(jnp.where(passed, inclusive, -before_own), axis=0, keepdims=True)
    stop = jnp.min(jnp.where(passed, 1e6, inclusive), axis=0, keepdims=True)
    child = target - start
    slot_f = lax.broadcasted_iota(jnp.int32, (window, LANES), 0).astype(F32)
    one_hot = jnp.where(slot_f == parent, 1.0, 0.0).astype(jnp.bfloat16)
    refined = jnp.where((stop - start) > 2.0, 1.0, 0.0)
    first_bit = jnp.where((child == 1.0) | (child == 3.0), 1.0, 0.0)
    second_bit = jnp.where(child >= 2.0, 1.0, 0.0)
    return one_hot, refined, first_bit, second_bit


def face_kernel(scalar_ref, weights_ref, staged_ref, faces_ref, one_hot_ref, flags_ref, dup_ref):
    one_hot, refined, first_bit, second_bit = lane_plan(scalar_ref[0], weights_ref)
    one_hot_ref[...] = one_hot
    flags_ref[...] = jnp.concatenate(
        [refined, first_bit, second_bit, jnp.zeros((5, LANES), F32)], axis=0
    )
    lines = staged_ref[0 : 8 * B]
    picked = jnp.dot(lines, one_hot, preferred_element_type=F32)
    half = B // 2
    bits = (first_bit > 0.0, second_bit > 0.0)
    for k in range(4):
        base = 4 * B * (k // 2)
        along, side = bits[1 - k // 2], bits[k // 2]
        line = [picked[base + i * B : base + (i + 1) * B] for i in range(4)]
        low, high, plain = ((line[0], line[2], line[0]), (line[1], line[3], line[3]))[k % 2]
        chosen = jnp.where(side, high, low)
        chosen = jnp.where(along, chosen[half:], chosen[:half])
        dup_ref[pl.ds(k * B, half, stride=2)] = chosen
        dup_ref[pl.ds(k * B + 1, half, stride=2)] = chosen
        coefficient = jnp.where(refined > 0.0, dup_ref[face(k)], plain)
        lanes = slice((k // 2) * LANES, (k // 2 + 1) * LANES)
        high, middle, low = (staged_ref[face(8 + 2 * i + k % 2), lanes].astype(F32) for i in range(3))
        right = high + (middle + low)
        faces_ref[face(k)] = right / (4.0 + coefficient) * (1.0 / THETA)


def sweep(field_ref, finish):
    edge = lax.broadcasted_iota(jnp.int32, (B, LANES), 0)
    is_first, is_last = edge == 0, edge == B - 1

    def plane(index, position):
        start = pl.multiple_of(index * B, B)
        at = pl.ds(start, B)
        centre = field_ref[at]
        if position == 0:
            total = field_ref[pl.ds((index + 1) * B, B)]
            left = pltpu.roll(centre, 1, 0)
        else:
            total = field_ref[pl.ds(pl.multiple_of((index - 1) * B, B), B)]
            left = field_ref[pl.ds(index * B - 1, B)]
        if position == 1:
            total = total + field_ref[pl.ds(pl.multiple_of((index + 1) * B, B), B)]
        if position == 2:
            right = pltpu.roll(centre, B - 1, 0)
        else:
            right = field_ref[pl.ds(index * B + 1, B)]
        total = total + jnp.where(is_first, 0.0, left) + jnp.where(is_last, 0.0, right)
        finish(at, centre, total)

    plane(0, 0)

    def step(index, carry):
        plane(index, 1)
        return carry

    lax.fori_loop(1, B - 1, step, 0, unroll=2)
    plane(B - 1, 2)


def build_kernel(prev_ref, own_ref, right_in, one_hot_ref, flags_ref, s_ref, inv_ref, diag_ref, part_ref, part_faces_ref, inv_faces_ref, right_ref, pick_ref, dup_ref, sem):
    read = pltpu.make_async_copy(right_in, right_ref, sem)
    read.start()
    chunk = ROWS // 8
    one_hot = one_hot_ref[...]
    refined, first_bit, second_bit = (flags_ref[i : i + 1] > 0.0 for i in range(3))

    def pick(step, carry):
        at = pl.ds(pl.multiple_of(step * chunk, chunk), chunk)
        both = jnp.concatenate([prev_ref[at], own_ref[at]], axis=1)
        pick_ref[at] = jnp.dot(both, one_hot, preferred_element_type=F32)
        return carry

    lax.fori_loop(0, ROWS // chunk, pick, 0, unroll=2)
    read.wait()
    half = B // 2

    def leaf(row, carry):
        low = pick_ref[pl.ds(pl.multiple_of(row * B, B), B)]
        high = pick_ref[pl.ds(pl.multiple_of((row + half) * B, B), B)]
        chosen = jnp.where(first_bit, high, low)
        chosen = jnp.where(second_bit, chosen[half:], chosen[:half])
        slot = pl.multiple_of((row % 2) * B, B)
        dup_ref[pl.ds(slot, half, stride=2)] = chosen
        dup_ref[pl.ds(slot + 1, half, stride=2)] = chosen
        doubled = dup_ref[pl.ds(slot, B)]
        for k in range(2):
            at = pl.ds(pl.multiple_of((2 * row + k) * B, B), B)
            diag = 4.0 + jnp.where(refined, doubled, pick_ref[at])
            inv = 1.0 / diag
            diag_ref[at] = diag
            inv_ref[at] = inv
            s_ref[at] = right_ref[at] * inv * (1.0 / THETA)
        return carry

    lax.fori_loop(0, half, leaf, 0, unroll=2)

    def finish(at, centre, total):
        part_ref[at] = (1.0 + C_1 + K_1 * (THETA - 1.0)) * centre + K_1 * (inv_ref[at] * total)

    sweep(s_ref, finish)
    for k, at in enumerate(FACE_SLICES):
        part_faces_ref[face(k)] = part_ref[at]
        inv_faces_ref[face(k)] = inv_ref[at]


def fill_ghosts(scalar_ref, source_refs, first_ref, second_ref, kind_ref, ghost_ref, pair_ref):
    position = scalar_ref[0]
    half = B // 2
    for side in range(4):
        kind = kind_ref[side : side + 1]
        values = []
        for index_ref in (first_ref, second_ref):
            index = index_ref[side : side + 1]
            offset = lax.shift_right_logical(index, 7) - position
            lane = jnp.broadcast_to(index & (LANES - 1), (B, LANES))
            value = jnp.zeros((B, LANES), F32)
            for i, source_ref in enumerate(source_refs):
                taken = jnp.take_along_axis(
                    source_ref[face(side ^ 1)], lane, axis=1, mode="promise_in_bounds"
                )
                value = jnp.where(offset == scalar_ref[1 + i], taken, value)
            values.append(value)
        leading, second = values
        at = side * 4 * B
        pair_ref[at : at + B] = leading
        pair_ref[at + B : at + 2 * B] = second
        mean_low = (pair_ref[pl.ds(at, half, stride=2)] + pair_ref[pl.ds(at + 1, half, stride=2)]) * 0.5
        mean_high = (
            pair_ref[pl.ds(at + B, half, stride=2)] + pair_ref[pl.ds(at + B + 1, half, stride=2)]
        ) * 0.5
        for part in range(2):
            for odd in range(2):
                pair_ref[pl.ds(at + (2 + part) * B + odd, half, stride=2)] = leading[
                    part * half : (part + 1) * half
                ]
        ghost = jnp.where(kind == 4, jnp.concatenate([mean_low, mean_high], axis=0), 0.0)
        ghost = jnp.where(kind == 1, leading, ghost)
        ghost = jnp.where(kind == 2, pair_ref[at + 2 * B : at + 3 * B], ghost)
        ghost = jnp.where(kind == 3, pair_ref[at + 3 * B : at + 4 * B], ghost)
        ghost_ref[face(side)] = ghost


CORNERS = (
    ((0, 0), (2, 0)),
    ((0, B - 1), (3, 0)),
    ((1, 0), (2, B - 1)),
    ((1, B - 1), (3, B - 1)),
)


def step_faces_kernel(scale, scalar_ref, own_ref, *refs):
    sources, (first_ref, second_ref, kind_ref, part_ref, inv_ref, out_ref, ghost_ref, sum_ref, pair_ref) = (
        (own_ref, *refs[:4]),
        refs[4:],
    )
    fill_ghosts(scalar_ref, sources, first_ref, second_ref, kind_ref, ghost_ref, pair_ref)
    sum_ref[...] = ghost_ref[...]
    for one, two in CORNERS:
        for (at_face, at_row), (of_face, of_row) in ((one, two), (two, one)):
            at, of = at_face * B + at_row, of_face * B + of_row
            sum_ref[at : at + 1] = sum_ref[at : at + 1] + ghost_ref[of : of + 1]
    out_ref[...] = part_ref[...] + scale * (inv_ref[...] * sum_ref[...])


def step_block_kernel(faces_ref, old_ref, u_ref, inv_ref, v_ref, part_ref, part_faces_ref):
    for k, at in enumerate(FACE_SLICES):
        v_ref[at] = faces_ref[face(k)]

    def finish(at, centre, total):
        part_ref[at] = (
            (1.0 + C_2 - K_2) * centre + (K_2 * THETA - C_2) * u_ref[at] + K_2 * (inv_ref[at] * total)
        )

    sweep(v_ref, finish)
    for k, at in enumerate(FACE_SLICES):
        part_faces_ref[face(k)] = part_ref[at]


def last_block_kernel(faces_ref, old_ref, right_ref, diag_ref, v_ref, out_ref, residual_ref, edge_ref, part_ref, sems):
    for k, at in enumerate(FACE_SLICES):
        v_ref[at] = faces_ref[face(k)]
    write = pltpu.make_async_copy(v_ref, out_ref, sems.at[0])
    write.start()

    def finish(at, centre, total):
        part_ref[at] = right_ref[at] - diag_ref[at] * centre + total

    sweep(v_ref, finish)
    write_residual = pltpu.make_async_copy(part_ref, residual_ref, sems.at[1])
    write_residual.start()
    edge_ref[0:B] = part_ref[0:B]
    edge_ref[B : 2 * B] = part_ref[ROWS - B : ROWS]
    for plane in range(B):
        for k, tile in enumerate((0, B - 8)):
            to = 2 * B + k * 8 * B + plane * 8
            edge_ref[to : to + 8] = part_ref[plane * B + tile : plane * B + tile + 8]
    write.wait()
    write_residual.wait()


def last_faces_kernel(scalar_ref, own_ref, *refs):
    sources, refs = (own_ref, *refs[:4]), refs[4:]
    first_ref, second_ref, kind_ref, edge_ref, _, out_ref, ghost_ref, pair_ref, sum_ref, sems = refs
    fill_ghosts(scalar_ref, sources, first_ref, second_ref, kind_ref, ghost_ref, pair_ref)
    sum_ref[...] = edge_ref[...]
    sum_ref[0 : 2 * B] = sum_ref[0 : 2 * B] + ghost_ref[0 : 2 * B]
    for (at_face, at_row), (of_face, of_row) in CORNERS:
        at, of = at_face * B + at_row, of_face * B + of_row
        sum_ref[at : at + 1] = sum_ref[at : at + 1] + ghost_ref[of : of + 1]
    copies = []
    for k in range(2):
        tiles = 2 * B + k * 8 * B
        at = pl.ds(tiles + 7 * k, B, stride=8)
        sum_ref[at] = sum_ref[at] + ghost_ref[face(2 + k)]
        copies.append((face(k), pl.ds(k * (ROWS - B), B)))
    copies = [
        pltpu.make_async_copy(sum_ref.at[of], out_ref.at[to], sems.at[k]) for k, (of, to) in enumerate(copies)
    ]
    cells = out_ref.reshape(B, B, LANES)
    for k in range(2):
        tiles = sum_ref.at[pl.ds(2 * B + k * 8 * B + 8, 8 * (B - 2))].reshape(B - 2, 8, LANES)
        copies.append(
            pltpu.make_async_copy(tiles, cells.at[pl.ds(1, B - 2), pl.ds(k * (B - 8), 8)], sems.at[2 + k])
        )
    for copy in copies:
        copy.start()
    for copy in copies:
        copy.wait()


def swap(value, axis, parity):
    count = lax.axis_size(axis)
    pairs = []
    for low in range(parity, count - 1, 2):
        pairs += [(low, low + 1), (low + 1, low)]
    return lax.ppermute(value, axis, pairs)


def exchange(faces):
    received = [swap(faces, "sfc", 0), swap(faces, "grp", 0), swap(faces, "grp", 1), swap(faces, "sfc", 1)]
    return [(array, VMEM) for array in (faces, *received)]


def body(old_coef, refine_flags, counts, right_side, nbr_first, nbr_second, face_kind):
    grp, sfc = lax.axis_index("grp"), lax.axis_index("sfc")
    n_sfc = lax.axis_size("sfc")
    devices = lax.axis_size(AXES)
    position = grp * n_sfc + sfc
    right = right_side.reshape(ROWS, LANES)
    flags = refine_flags.reshape(1, LANES)
    own = old_coef.reshape(ROWS, LANES)
    prev = lax.ppermute(own, AXES, [(i, i + 1) for i in range(devices - 1)])
    (spread,) = call(
        weights_kernel,
        [(counts, SMEM), (flags, VMEM)],
        [(kept(devices, jnp.int32), VMEM)],
    )
    weights = lax.all_to_all(spread, AXES, 0, 0, tiled=True)
    even_sfc, even_grp = 1 - 2 * (sfc % 2), n_sfc * (1 - 2 * (grp % 2))
    scalars = jnp.stack([position, 0, even_sfc, even_grp, -even_grp, -even_sfc]).astype(jnp.int32)

    staged, prev, own = call(
        stage_kernel,
        [(prev, ANY), (own, HBM), (right_side, HBM)],
        [(kept(14 * B, jnp.bfloat16, 2 * LANES), VMEM)] + [(kept(ROWS, jnp.bfloat16), VMEM)] * 2,
        [vmem(ROWS), pltpu.VMEM((2, B, 8, LANES), F32), vmem(4 * B), pltpu.SemaphoreType.DMA((6,))],
        flops=8_000_000,
    )
    faces, one_hot, flags = call(
        face_kernel,
        [(scalars, SMEM), (weights, FREE), (staged, FREE)],
        [(kept(4 * B), VMEM), (kept(2 * LANES, jnp.bfloat16), VMEM), (kept(8), VMEM)],
        [vmem(4 * B)],
    )
    neighbours = exchange(faces)
    s1, inv, diag, part, part_faces, inv_faces, right = call(
        build_kernel,
        [(prev, VMEM), (own, VMEM), (right, HBM), (one_hot, VMEM), (flags, VMEM)],
        [(kept(ROWS), VMEM)] * 4 + [(kept(4 * B), VMEM)] * 2 + [(kept(ROWS), VMEM)],
        [vmem(ROWS), vmem(2 * B), pltpu.SemaphoreType.DMA],
        flops=8_000_000,
    )
    plan = [(nbr_first, VMEM), (nbr_second, VMEM), (face_kind, VMEM)]
    ghost_scratch = [vmem(4 * B), vmem(4 * B), vmem(16 * B)]
    (faces,) = call(
        functools.partial(step_faces_kernel, K_1),
        [(scalars, SMEM), *neighbours, *plan, (part_faces, VMEM), (inv_faces, VMEM)],
        [(kept(4 * B), VMEM)],
        ghost_scratch,
    )
    neighbours = exchange(faces)
    _, part, part_faces = call(
        step_block_kernel,
        [(faces, VMEM), (part, VMEM), (s1, VMEM), (inv, VMEM)],
        [(kept(ROWS), VMEM), (kept(ROWS), VMEM), (kept(4 * B), VMEM)],
        aliases={1: 0},
        flops=8_000_000,
    )
    (faces,) = call(
        functools.partial(step_faces_kernel, K_2),
        [(scalars, SMEM), *neighbours, *plan, (part_faces, VMEM), (inv_faces, VMEM)],
        [(kept(4 * B), VMEM)],
        ghost_scratch,
    )
    neighbours = exchange(faces)
    _, iterate, residual, edges = call(
        last_block_kernel,
        [(faces, VMEM), (part, VMEM), (right, VMEM), (diag, VMEM)],
        [(kept(ROWS), VMEM), (in_hbm((ROWS, LANES)), HBM), (in_hbm((ROWS, LANES)), HBM), (kept(18 * B), VMEM)],
        [vmem(ROWS), pltpu.SemaphoreType.DMA((2,))],
        aliases={1: 0},
        flops=8_000_000,
    )
    (residual,) = call(
        last_faces_kernel,
        [(scalars, SMEM), *neighbours, *plan, (edges, VMEM), (residual, HBM)],
        [(in_hbm((ROWS, LANES)), HBM)],
        [vmem(4 * B), vmem(16 * B), vmem(18 * B), pltpu.SemaphoreType.DMA((4,))],
        aliases={10: 0},
    )
    return iterate.reshape(B, B, LANES), residual.reshape(B, B, LANES)


def solution(mesh):
    leaves, lines = P(None, None, AXES), P(None, AXES)
    return jax.shard_map(
        body,
        mesh=mesh,
        in_specs=(leaves, P(AXES), P(AXES), leaves, lines, lines, lines),
        out_specs=(leaves, leaves),
        check_vma=False,
    )
```

```python
import functools

import jax
import jax.numpy as jnp
from jax import lax
from jax.experimental import pallas as pl
from jax.experimental.pallas import tpu as pltpu
from jax.sharding import PartitionSpec as P

LOWER_BOUND = 0.3
UPPER_BOUND = 1.9
B = 64
ROWS = B * B
LANES = 128
AXES = ("grp", "sfc")

THETA = (UPPER_BOUND + LOWER_BOUND) / 2.0
DELTA = (UPPER_BOUND - LOWER_BOUND) / 2.0
SIGMA = THETA / DELTA
RHO_0 = 1.0 / SIGMA
RHO_1 = 1.0 / (2.0 * SIGMA - RHO_0)
RHO_2 = 1.0 / (2.0 * SIGMA - RHO_1)
C_1, K_1 = RHO_1 * RHO_0, 2.0 * RHO_1 / DELTA
C_2, K_2 = RHO_2 * RHO_1, 2.0 * RHO_2 / DELTA
SECOND = 1.0 + C_1 + K_1 * (THETA - 1.0)

F32 = jnp.float32
VMEM_LIMIT = 32 * 1024 * 1024


def placed(array, space):
    return array if space in (SMEM, ANY) else pltpu.with_memory_space_constraint(array, SPACES[space])


def vmem(rows, dtype=F32):
    return pltpu.VMEM((rows, LANES), dtype)


def kept(rows, dtype=F32, lanes=LANES):
    return pltpu.VMEM((rows, lanes), dtype)


def in_hbm(shape):
    return pltpu.HBM(shape, F32)


SMEM, VMEM, HBM, ANY = "smem", "vmem", "hbm", "any"
SPACES = {SMEM: pltpu.SMEM, VMEM: pltpu.VMEM, HBM: pltpu.HBM, ANY: pl.ANY}


def call(kernel, operands, outs, scratch=(), aliases=None, flops=1_000_000):
    specs = [pl.BlockSpec(memory_space=SPACES[space]) for _, space in operands]
    return pl.pallas_call(
        kernel,
        out_shape=[shape for shape, _ in outs],
        in_specs=specs,
        out_specs=[pl.BlockSpec(memory_space=SPACES[space]) for _, space in outs],
        scratch_shapes=list(scratch),
        input_output_aliases=aliases or {},
        compiler_params=pltpu.CompilerParams(vmem_limit_bytes=VMEM_LIMIT),
        cost_estimate=pl.CostEstimate(flops=flops, bytes_accessed=flops, transcendentals=0),
    )(*[placed(array, space) for array, space in operands])


FACE_SLICES = (pl.ds(0, B), pl.ds(ROWS - B, B), pl.ds(0, B, stride=B), pl.ds(B - 1, B, stride=B))
LINES = (0, B // 2 - 1, B // 2, B - 1)


def face(index):
    return pl.ds(index * B, B)


def weights_kernel(count_ref, flags_ref, out_ref):
    slot = lax.broadcasted_iota(jnp.int32, (1, LANES), 1)
    weight = jnp.where(slot < count_ref[0], 1 + 3 * flags_ref[...], 0)
    out_ref[...] = jnp.broadcast_to(weight, out_ref.shape)


LINES_AT = ROWS
RIGHT_AT = LINES_AT + 16 * B
HELD = RIGHT_AT + 12 * B


def stage_kernel(prev_in, own_in, right_in, prev_ref, held_ref, wide_ref, edge_ref, faces_ref, sems):
    own_ref = held_ref.at[pl.ds(0, ROWS)]
    blocks = [
        pltpu.make_async_copy(of, to, sems.at[k])
        for k, (of, to) in enumerate(((prev_in, prev_ref), (own_in, own_ref)))
    ]
    reads = []
    for k in range(2):
        reads.append(pltpu.make_async_copy(right_in.at[k * (B - 1)], faces_ref.at[face(k)], sems.at[2 + k]))
        of = right_in.at[:, pl.ds(k * (B - 8), 8)]
        reads.append(pltpu.make_async_copy(of, edge_ref.at[k], sems.at[4 + k]))
    for read in (*blocks, *reads):
        read.start()
    for side, ref in enumerate((prev_ref, held_ref)):
        blocks[side].wait()
        wide_ref[...] = ref[0:ROWS].astype(F32)
        for k, line in enumerate(LINES):
            at = LINES_AT + (8 * side + k) * B
            held_ref[at : at + B] = ref[face(line)]
            at = at + 4 * B
            held_ref[at : at + B] = wide_ref[pl.ds(line, B, stride=B)].astype(jnp.bfloat16)
    for read in reads:
        read.wait()
    for k in range(2):
        faces_ref[face(2 + k)] = edge_ref[k, :, 7 * k, :]
    left = faces_ref[...]
    for piece in range(3):
        part = left.astype(jnp.bfloat16)
        at = RIGHT_AT + 4 * piece * B
        held_ref[at : at + 4 * B] = part
        left = left - part.astype(F32)


def lane_plan(position, weights_ref):
    rows = lax.broadcasted_iota(jnp.int32, weights_ref.shape, 0)
    before = jnp.where(rows < position, weights_ref[...], 0).astype(F32)
    made = jnp.sum(jnp.sum(before, axis=0, keepdims=True), axis=1, keepdims=True)
    drift = made - (position * LANES).astype(F32)
    own = weights_ref[pl.ds(position, 1), :].astype(F32)
    prev = weights_ref[pl.ds(jnp.maximum(position - 1, 0), 1), :].astype(F32)
    prev = jnp.where(position > 0, prev, 0.0)
    window = 2 * LANES
    spread = jnp.broadcast_to(jnp.concatenate([prev, own], axis=1), (LANES, window)).astype(jnp.bfloat16)
    slot = lax.broadcasted_iota(jnp.int32, (window, window), 0)
    other = lax.broadcasted_iota(jnp.int32, (window, window), 1)
    lower = jnp.where(other <= slot, 1.0, 0.0).astype(jnp.bfloat16)
    inclusive = lax.dot_general(
        lower, spread, (((1,), (1,)), ((), ())), preferred_element_type=F32
    )
    before_own = inclusive[LANES - 1 : LANES]
    inclusive = inclusive - before_own
    target = lax.broadcasted_iota(jnp.int32, (1, LANES), 1).astype(F32) - drift
    passed = inclusive <= target
    parent = jnp.sum(jnp.where(passed, 1.0, 0.0), axis=0, keepdims=True)
    start = jnp.max(jnp.where(passed, inclusive, -before_own), axis=0, keepdims=True)
    stop = jnp.min(jnp.where(passed, 1e6, inclusive), axis=0, keepdims=True)
    child = target - start
    slot_f = lax.broadcasted_iota(jnp.int32, (window, LANES), 0).astype(F32)
    one_hot = jnp.where(slot_f == parent, 1.0, 0.0).astype(jnp.bfloat16)
    refined = jnp.where((stop - start) > 2.0, 1.0, 0.0)
    first_bit = jnp.where((child == 1.0) | (child == 3.0), 1.0, 0.0)
    second_bit = jnp.where(child >= 2.0, 1.0, 0.0)
    return one_hot, refined, first_bit, second_bit


def face_kernel(scalar_ref, weights_ref, held_ref, faces_ref, one_hot_ref, flags_ref, dup_ref):
    one_hot, refined, first_bit, second_bit = lane_plan(scalar_ref[0], weights_ref)
    one_hot_ref[...] = one_hot
    flags_ref[...] = jnp.concatenate(
        [refined, first_bit, second_bit, jnp.zeros((5, LANES), F32)], axis=0
    )
    lines = jnp.concatenate(
        [held_ref[LINES_AT : LINES_AT + 8 * B], held_ref[LINES_AT + 8 * B : RIGHT_AT]], axis=1
    )
    picked = jnp.dot(lines, one_hot, preferred_element_type=F32)
    half = B // 2
    bits = (first_bit > 0.0, second_bit > 0.0)
    for k in range(4):
        base = 4 * B * (k // 2)
        along, side = bits[1 - k // 2], bits[k // 2]
        line = [picked[base + i * B : base + (i + 1) * B] for i in range(4)]
        low, high, plain = ((line[0], line[2], line[0]), (line[1], line[3], line[3]))[k % 2]
        chosen = jnp.where(side, high, low)
        chosen = jnp.where(along, chosen[half:], chosen[:half])
        dup_ref[pl.ds(k * B, half, stride=2)] = chosen
        dup_ref[pl.ds(k * B + 1, half, stride=2)] = chosen
        coefficient = jnp.where(refined > 0.0, dup_ref[face(k)], plain)
        high, middle, low = (
            held_ref[RIGHT_AT + (4 * i + k) * B : RIGHT_AT + (4 * i + k + 1) * B].astype(F32) for i in range(3)
        )
        right = high + (middle + low)
        faces_ref[face(k)] = right / (4.0 + coefficient) * (1.0 / THETA)


def sweep(field_ref, finish, pieces=1, after=None):
    edge = lax.broadcasted_iota(jnp.int32, (B, LANES), 0)
    is_first, is_last = edge == 0, edge == B - 1

    def plane(index, position):
        start = pl.multiple_of(index * B, B)
        at = pl.ds(start, B)
        centre = field_ref[at]
        if position == 0:
            total = field_ref[pl.ds((index + 1) * B, B)]
            left = pltpu.roll(centre, 1, 0)
        else:
            total = field_ref[pl.ds(pl.multiple_of((index - 1) * B, B), B)]
            left = field_ref[pl.ds(index * B - 1, B)]
        if position == 1:
            total = total + field_ref[pl.ds(pl.multiple_of((index + 1) * B, B), B)]
        if position == 2:
            right = pltpu.roll(centre, B - 1, 0)
        else:
            right = field_ref[pl.ds(index * B + 1, B)]
        total = total + jnp.where(is_first, 0.0, left) + jnp.where(is_last, 0.0, right)
        finish(at, centre, total)

    def step(index, carry):
        plane(index, 1)
        return carry

    plane(0, 0)
    bounds = [max(1, piece * B // pieces) for piece in range(pieces)] + [B - 1]
    for piece in range(pieces):
        lax.fori_loop(bounds[piece], bounds[piece + 1], step, 0, unroll=2)
        if piece == pieces - 1:
            plane(B - 1, 2)
        if after is not None:
            after(piece)


def build_kernel(prev_ref, own_ref, right_in, one_hot_ref, flags_ref, s_ref, inv_ref, diag_ref, part_faces_ref, inv_faces_ref, right_ref, pick_ref, dup_ref, sem):
    read = pltpu.make_async_copy(right_in, right_ref, sem)
    read.start()
    chunk = ROWS // 8
    one_hot = one_hot_ref[...]
    refined, first_bit, second_bit = (flags_ref[i : i + 1] > 0.0 for i in range(3))

    def pick(step, carry):
        at = pl.ds(pl.multiple_of(step * chunk, chunk), chunk)
        both = jnp.concatenate([prev_ref[at], own_ref[at]], axis=1)
        pick_ref[at] = jnp.dot(both, one_hot, preferred_element_type=F32)
        return carry

    lax.fori_loop(0, ROWS // chunk, pick, 0, unroll=2)
    read.wait()
    half = B // 2

    def leaf(row, carry):
        low = pick_ref[pl.ds(pl.multiple_of(row * B, B), B)]
        high = pick_ref[pl.ds(pl.multiple_of((row + half) * B, B), B)]
        chosen = jnp.where(first_bit, high, low)
        chosen = jnp.where(second_bit, chosen[half:], chosen[:half])
        slot = pl.multiple_of((row % 2) * B, B)
        dup_ref[pl.ds(slot, half, stride=2)] = chosen
        dup_ref[pl.ds(slot + 1, half, stride=2)] = chosen
        doubled = dup_ref[pl.ds(slot, B)]
        for k in range(2):
            at = pl.ds(pl.multiple_of((2 * row + k) * B, B), B)
            diag = 4.0 + jnp.where(refined, doubled, pick_ref[at])
            inv = 1.0 / diag
            diag_ref[at] = diag
            inv_ref[at] = inv
            s_ref[at] = right_ref[at] * inv * (1.0 / THETA)
        return carry

    lax.fori_loop(0, half, leaf, 0, unroll=2)

    edge = lax.broadcasted_iota(jnp.int32, (B, LANES), 0)
    inside = (
        s_ref[pl.ds(B, B)],
        s_ref[pl.ds(ROWS - 2 * B, B)],
        s_ref[pl.ds(1, B, stride=B)],
        s_ref[pl.ds(B - 2, B, stride=B)],
    )
    for k, at in enumerate(FACE_SLICES):
        line, inv = s_ref[at], inv_ref[at]
        total = inside[k] + jnp.where(edge == 0, 0.0, pltpu.roll(line, 1, 0))
        total = total + jnp.where(edge == B - 1, 0.0, pltpu.roll(line, B - 1, 0))
        part_faces_ref[face(k)] = SECOND * line + K_1 * (inv * total)
        inv_faces_ref[face(k)] = inv


def gathered(scalar_ref, index, side, source_refs):
    offset = lax.shift_right_logical(index, 7) - scalar_ref[0]
    lane = jnp.broadcast_to(index & (LANES - 1), (B, LANES))
    value = jnp.zeros((B, LANES), F32)
    for number, ref in enumerate(source_refs):
        taken = jnp.take_along_axis(ref[face(side ^ 1)], lane, axis=1, mode="promise_in_bounds")
        value = jnp.where(offset == scalar_ref[1 + number], taken, value)
    return value


def fill_ghost(side, scalar_ref, source_refs, first_ref, second_ref, kind_ref, ghost_ref, pair_ref):
    half = B // 2
    kind = kind_ref[side : side + 1]
    leading, second = (
        gathered(scalar_ref, index_ref[side : side + 1], side, source_refs)
        for index_ref in (first_ref, second_ref)
    )
    at = side * 4 * B
    pair_ref[at : at + B] = leading
    pair_ref[at + B : at + 2 * B] = second
    mean_low = (pair_ref[pl.ds(at, half, stride=2)] + pair_ref[pl.ds(at + 1, half, stride=2)]) * 0.5
    mean_high = (
        pair_ref[pl.ds(at + B, half, stride=2)] + pair_ref[pl.ds(at + B + 1, half, stride=2)]
    ) * 0.5
    for part in range(2):
        for odd in range(2):
            pair_ref[pl.ds(at + (2 + part) * B + odd, half, stride=2)] = leading[
                part * half : (part + 1) * half
            ]
    ghost = jnp.where(kind == 4, jnp.concatenate([mean_low, mean_high], axis=0), 0.0)
    ghost = jnp.where(kind == 1, leading, ghost)
    ghost = jnp.where(kind == 2, pair_ref[at + 2 * B : at + 3 * B], ghost)
    ghost = jnp.where(kind == 3, pair_ref[at + 3 * B : at + 4 * B], ghost)
    ghost_ref[face(side)] = ghost


CORNERS = (
    ((0, 0), (2, 0)),
    ((0, B - 1), (3, 0)),
    ((1, 0), (2, B - 1)),
    ((1, B - 1), (3, B - 1)),
)


def step_faces_kernel(scale, scalar_ref, *refs):
    sources, plan, (part_ref, inv_ref, out_ref, ghost_ref, sum_ref, pair_ref) = refs[:5], refs[5:8], refs[8:]
    for side in range(4):
        fill_ghost(side, scalar_ref, sources, *plan, ghost_ref, pair_ref)
    sum_ref[...] = ghost_ref[...]
    for one, two in CORNERS:
        for (at_face, at_row), (of_face, of_row) in ((one, two), (two, one)):
            at, of = at_face * B + at_row, of_face * B + of_row
            sum_ref[at : at + 1] = sum_ref[at : at + 1] + ghost_ref[of : of + 1]
    out_ref[...] = part_ref[...] + scale * (inv_ref[...] * sum_ref[...])


def step_block_kernel(faces_ref, u_ref, inv_ref, part_ref, part_faces_ref, v_ref):
    def second(at, centre, total):
        v_ref[at] = SECOND * centre + K_1 * (inv_ref[at] * total)

    sweep(u_ref, second)
    for k, at in enumerate(FACE_SLICES):
        v_ref[at] = faces_ref[face(k)]

    def finish(at, centre, total):
        part_ref[at] = (
            (1.0 + C_2 - K_2) * centre + (K_2 * THETA - C_2) * u_ref[at] + K_2 * (inv_ref[at] * total)
        )

    sweep(v_ref, finish)
    for k, at in enumerate(FACE_SLICES):
        part_faces_ref[face(k)] = part_ref[at]


def last_block_kernel(faces_ref, old_ref, right_ref, diag_ref, v_ref, out_ref, residual_ref, edge_ref, part_ref, sems):
    for k, at in enumerate(FACE_SLICES):
        v_ref[at] = faces_ref[face(k)]
    writes = [pltpu.make_async_copy(v_ref, out_ref, sems.at[0])]
    writes[0].start()

    def finish(at, centre, total):
        part_ref[at] = right_ref[at] - diag_ref[at] * centre + total

    def write(quarter):
        at = pl.ds(quarter * (ROWS // 4), ROWS // 4)
        writes.append(pltpu.make_async_copy(part_ref.at[at], residual_ref.at[at], sems.at[1 + quarter]))
        writes[-1].start()

    sweep(v_ref, finish, 4, write)
    edge_ref[0:B] = part_ref[0:B]
    edge_ref[B : 2 * B] = part_ref[ROWS - B : ROWS]
    for plane in range(B):
        for k, tile in enumerate((0, B - 8)):
            to = 2 * B + k * 8 * B + plane * 8
            edge_ref[to : to + 8] = part_ref[plane * B + tile : plane * B + tile + 8]
    for copy in writes:
        copy.wait()


def last_faces_kernel(scalar_ref, *refs):
    sources, plan, refs = (refs[0], *refs[2:5], refs[1]), refs[5:8], refs[8:]
    edge_ref, _, out_ref, ghost_ref, pair_ref, sum_ref, sems = refs
    copies = []
    cells = out_ref.reshape(B, B, LANES)
    for k in range(2):
        tiles = 2 * B + k * 8 * B
        sum_ref[tiles : tiles + 8 * B] = edge_ref[tiles : tiles + 8 * B]
        fill_ghost(2 + k, scalar_ref, sources, *plan, ghost_ref, pair_ref)
        at = pl.ds(tiles + 7 * k, B, stride=8)
        sum_ref[at] = sum_ref[at] + ghost_ref[face(2 + k)]
        of = sum_ref.at[pl.ds(tiles + 8, 8 * (B - 2))].reshape(B - 2, 8, LANES)
        to = cells.at[pl.ds(1, B - 2), pl.ds(k * (B - 8), 8)]
        copies.append(pltpu.make_async_copy(of, to, sems.at[2 + k]))
        copies[-1].start()
    for k in range(2):
        fill_ghost(k, scalar_ref, sources, *plan, ghost_ref, pair_ref)
        sum_ref[face(k)] = edge_ref[face(k)] + ghost_ref[face(k)]
        for (at_face, at_row), (of_face, of_row) in CORNERS[2 * k : 2 * k + 2]:
            at, of = at_face * B + at_row, of_face * B + of_row
            sum_ref[at : at + 1] = sum_ref[at : at + 1] + ghost_ref[of : of + 1]
        to = out_ref.at[pl.ds(k * (ROWS - B), B)]
        copies.append(pltpu.make_async_copy(sum_ref.at[face(k)], to, sems.at[k]))
        copies[-1].start()
    for copy in copies:
        copy.wait()


def swap(value, axis, parity):
    count = lax.axis_size(axis)
    pairs = []
    for low in range(parity, count - 1, 2):
        pairs += [(low, low + 1), (low + 1, low)]
    return lax.ppermute(value, axis, pairs)


def exchange(faces):
    received = [swap(faces, "sfc", 1), swap(faces, "grp", 1), swap(faces, "grp", 0), swap(faces, "sfc", 0)]
    return [(array, VMEM) for array in (faces, *received)]


def body(old_coef, refine_flags, counts, right_side, nbr_first, nbr_second, face_kind):
    grp, sfc = lax.axis_index("grp"), lax.axis_index("sfc")
    n_sfc = lax.axis_size("sfc")
    devices = lax.axis_size(AXES)
    position = grp * n_sfc + sfc
    right = right_side.reshape(ROWS, LANES)
    own = old_coef.reshape(ROWS, LANES)
    prev = lax.ppermute(own, AXES, [(i, i + 1) for i in range(devices - 1)])
    (spread,) = call(
        weights_kernel,
        [(counts, SMEM), (refine_flags.reshape(1, LANES), VMEM)],
        [(kept(devices, jnp.int32), VMEM)],
    )
    weights = lax.all_to_all(spread, AXES, 0, 0, tiled=True)
    even_sfc, even_grp = 1 - 2 * (sfc % 2), n_sfc * (1 - 2 * (grp % 2))
    scalars = jnp.stack([position, 0, -even_sfc, -even_grp, even_grp, even_sfc]).astype(jnp.int32)

    prev, held = call(
        stage_kernel,
        [(prev, ANY), (own, HBM), (right_side, HBM)],
        [(kept(ROWS, jnp.bfloat16), VMEM), (kept(HELD, jnp.bfloat16), VMEM)],
        [vmem(ROWS), pltpu.VMEM((2, B, 8, LANES), F32), vmem(4 * B), pltpu.SemaphoreType.DMA((6,))],
        flops=8_000_000,
    )
    faces, one_hot, flags = call(
        face_kernel,
        [(scalars, SMEM), (weights, VMEM), (held, VMEM)],
        [(kept(4 * B), VMEM), (kept(2 * LANES, jnp.bfloat16), VMEM), (kept(8), VMEM)],
        [vmem(4 * B)],
    )
    neighbours = exchange(faces)
    s1, inv, diag, part_faces, inv_faces, right = call(
        build_kernel,
        [(prev, VMEM), (held, VMEM), (right, HBM), (one_hot, VMEM), (flags, VMEM)],
        [(kept(ROWS), VMEM)] * 3 + [(kept(4 * B), VMEM)] * 2 + [(kept(ROWS), VMEM)],
        [vmem(ROWS), vmem(2 * B), pltpu.SemaphoreType.DMA],
        flops=8_000_000,
    )
    plan = [(nbr_first, VMEM), (nbr_second, VMEM), (face_kind, VMEM)]
    ghost_scratch = [vmem(4 * B), vmem(4 * B), vmem(16 * B)]
    (faces,) = call(
        functools.partial(step_faces_kernel, K_1),
        [(scalars, SMEM), *neighbours, *plan, (part_faces, VMEM), (inv_faces, VMEM)],
        [(kept(4 * B), VMEM)],
        ghost_scratch,
    )
    neighbours = exchange(faces)
    part, part_faces = call(
        step_block_kernel,
        [(faces, VMEM), (s1, VMEM), (inv, VMEM)],
        [(kept(ROWS), VMEM), (kept(4 * B), VMEM)],
        [vmem(ROWS)],
        flops=8_000_000,
    )
    (faces,) = call(
        functools.partial(step_faces_kernel, K_2),
        [(scalars, SMEM), *neighbours, *plan, (part_faces, VMEM), (inv_faces, VMEM)],
        [(kept(4 * B), VMEM)],
        ghost_scratch,
    )
    neighbours = exchange(faces)
    neighbours = [neighbours[0], neighbours[4], *neighbours[1:4]]
    whole = (in_hbm((ROWS, LANES)), HBM)
    _, iterate, residual, edges = call(
        last_block_kernel,
        [(faces, VMEM), (part, VMEM), (right, VMEM), (diag, VMEM)],
        [(kept(ROWS), VMEM), whole, whole, (kept(18 * B), VMEM)],
        [vmem(ROWS), pltpu.SemaphoreType.DMA((5,))],
        aliases={1: 0},
        flops=8_000_000,
    )
    (residual,) = call(
        last_faces_kernel,
        [(scalars, SMEM), *neighbours, *plan, (edges, VMEM), (residual, HBM)],
        [whole],
        [vmem(4 * B), vmem(16 * B), vmem(18 * B), pltpu.SemaphoreType.DMA((4,))],
        aliases={10: 0},
    )
    return iterate.reshape(B, B, LANES), residual.reshape(B, B, LANES)


def solution(mesh):
    leaves, lines = P(None, None, AXES), P(None, AXES)
    return jax.shard_map(
        body,
        mesh=mesh,
        in_specs=(leaves, P(AXES), P(AXES), leaves, lines, lines, lines),
        out_specs=(leaves, leaves),
        check_vma=False,
    )
```

```python
import functools

import jax
import jax.numpy as jnp
from jax import lax
from jax.experimental import pallas as pl
from jax.experimental.pallas import tpu as pltpu
from jax.sharding import PartitionSpec as P

LOWER_BOUND = 0.3
UPPER_BOUND = 1.9
B = 64
ROWS = B * B
LANES = 128
AXES = ("grp", "sfc")

THETA = (UPPER_BOUND + LOWER_BOUND) / 2.0
DELTA = (UPPER_BOUND - LOWER_BOUND) / 2.0
SIGMA = THETA / DELTA
RHO_0 = 1.0 / SIGMA
RHO_1 = 1.0 / (2.0 * SIGMA - RHO_0)
RHO_2 = 1.0 / (2.0 * SIGMA - RHO_1)
C_1, K_1 = RHO_1 * RHO_0, 2.0 * RHO_1 / DELTA
C_2, K_2 = RHO_2 * RHO_1, 2.0 * RHO_2 / DELTA
SECOND = 1.0 + C_1 + K_1 * (THETA - 1.0)

F32 = jnp.float32
VMEM_LIMIT = 32 * 1024 * 1024


def placed(array, space):
    return array if space in (SMEM, ANY) else pltpu.with_memory_space_constraint(array, SPACES[space])


def vmem(rows, dtype=F32):
    return pltpu.VMEM((rows, LANES), dtype)


def kept(rows, dtype=F32, lanes=LANES):
    return pltpu.VMEM((rows, lanes), dtype)


def in_hbm(shape):
    return pltpu.HBM(shape, F32)


SMEM, VMEM, HBM, ANY = "smem", "vmem", "hbm", "any"
SPACES = {SMEM: pltpu.SMEM, VMEM: pltpu.VMEM, HBM: pltpu.HBM, ANY: pl.ANY}


def call(kernel, operands, outs, scratch=(), aliases=None, flops=1_000_000):
    specs = [pl.BlockSpec(memory_space=SPACES[space]) for _, space in operands]
    return pl.pallas_call(
        kernel,
        out_shape=[shape for shape, _ in outs],
        in_specs=specs,
        out_specs=[pl.BlockSpec(memory_space=SPACES[space]) for _, space in outs],
        scratch_shapes=list(scratch),
        input_output_aliases=aliases or {},
        compiler_params=pltpu.CompilerParams(vmem_limit_bytes=VMEM_LIMIT),
        cost_estimate=pl.CostEstimate(flops=flops, bytes_accessed=flops, transcendentals=0),
    )(*[placed(array, space) for array, space in operands])


FACE_SLICES = (pl.ds(0, B), pl.ds(ROWS - B, B), pl.ds(0, B, stride=B), pl.ds(B - 1, B, stride=B))
LINES = (0, B // 2 - 1, B // 2, B - 1)


def face(index):
    return pl.ds(index * B, B)


def weights_kernel(count_ref, flags_ref, out_ref):
    slot = lax.broadcasted_iota(jnp.int32, (1, LANES), 1)
    weight = jnp.where(slot < count_ref[0], 1 + 3 * flags_ref[...], 0)
    out_ref[...] = jnp.broadcast_to(weight, out_ref.shape)


LINES_AT = ROWS
RIGHT_AT = LINES_AT + 16 * B
HELD = RIGHT_AT + 12 * B


def stage_kernel(prev_in, own_in, right_in, prev_ref, held_ref, wide_ref, edge_ref, faces_ref, sems):
    own_ref = held_ref.at[pl.ds(0, ROWS)]
    blocks = [
        pltpu.make_async_copy(of, to, sems.at[k])
        for k, (of, to) in enumerate(((prev_in, prev_ref), (own_in, own_ref)))
    ]
    reads = []
    for k in range(2):
        reads.append(pltpu.make_async_copy(right_in.at[k * (B - 1)], faces_ref.at[face(k)], sems.at[2 + k]))
        of = right_in.at[:, pl.ds(k * (B - 8), 8)]
        reads.append(pltpu.make_async_copy(of, edge_ref.at[k], sems.at[4 + k]))
    for read in (*blocks, *reads):
        read.start()
    for side, ref in enumerate((prev_ref, held_ref)):
        blocks[side].wait()
        wide_ref[...] = ref[0:ROWS].astype(F32)
        for k, line in enumerate(LINES):
            at = LINES_AT + (8 * side + k) * B
            held_ref[at : at + B] = ref[face(line)]
            at = at + 4 * B
            held_ref[at : at + B] = wide_ref[pl.ds(line, B, stride=B)].astype(jnp.bfloat16)
    for read in reads:
        read.wait()
    for k in range(2):
        faces_ref[face(2 + k)] = edge_ref[k, :, 7 * k, :]
    left = faces_ref[...]
    for piece in range(3):
        part = left.astype(jnp.bfloat16)
        at = RIGHT_AT + 4 * piece * B
        held_ref[at : at + 4 * B] = part
        left = left - part.astype(F32)


def lane_plan(position, weights_ref):
    rows = lax.broadcasted_iota(jnp.int32, weights_ref.shape, 0)
    before = jnp.where(rows < position, weights_ref[...], 0).astype(F32)
    made = jnp.sum(jnp.sum(before, axis=0, keepdims=True), axis=1, keepdims=True)
    drift = made - (position * LANES).astype(F32)
    own = weights_ref[pl.ds(position, 1), :].astype(F32)
    prev = weights_ref[pl.ds(jnp.maximum(position - 1, 0), 1), :].astype(F32)
    prev = jnp.where(position > 0, prev, 0.0)
    window = 2 * LANES
    spread = jnp.broadcast_to(jnp.concatenate([prev, own], axis=1), (LANES, window)).astype(jnp.bfloat16)
    slot = lax.broadcasted_iota(jnp.int32, (window, window), 0)
    other = lax.broadcasted_iota(jnp.int32, (window, window), 1)
    lower = jnp.where(other <= slot, 1.0, 0.0).astype(jnp.bfloat16)
    inclusive = lax.dot_general(
        lower, spread, (((1,), (1,)), ((), ())), preferred_element_type=F32
    )
    before_own = inclusive[LANES - 1 : LANES]
    inclusive = inclusive - before_own
    target = lax.broadcasted_iota(jnp.int32, (1, LANES), 1).astype(F32) - drift
    passed = inclusive <= target
    parent = jnp.sum(jnp.where(passed, 1.0, 0.0), axis=0, keepdims=True)
    start = jnp.max(jnp.where(passed, inclusive, -before_own), axis=0, keepdims=True)
    stop = jnp.min(jnp.where(passed, 1e6, inclusive), axis=0, keepdims=True)
    child = target - start
    slot_f = lax.broadcasted_iota(jnp.int32, (window, LANES), 0).astype(F32)
    one_hot = jnp.where(slot_f == parent, 1.0, 0.0).astype(jnp.bfloat16)
    refined = jnp.where((stop - start) > 2.0, 1.0, 0.0)
    first_bit = jnp.where((child == 1.0) | (child == 3.0), 1.0, 0.0)
    second_bit = jnp.where(child >= 2.0, 1.0, 0.0)
    return one_hot, refined, first_bit, second_bit


def face_kernel(scalar_ref, weights_ref, held_ref, faces_ref, one_hot_ref, flags_ref, dup_ref):
    one_hot, refined, first_bit, second_bit = lane_plan(scalar_ref[0], weights_ref)
    one_hot_ref[...] = one_hot
    flags_ref[...] = jnp.concatenate(
        [refined, first_bit, second_bit, jnp.zeros((5, LANES), F32)], axis=0
    )
    lines = jnp.concatenate(
        [held_ref[LINES_AT : LINES_AT + 8 * B], held_ref[LINES_AT + 8 * B : RIGHT_AT]], axis=1
    )
    picked = jnp.dot(lines, one_hot, preferred_element_type=F32)
    half = B // 2
    bits = (first_bit > 0.0, second_bit > 0.0)
    for k in range(4):
        base = 4 * B * (k // 2)
        along, side = bits[1 - k // 2], bits[k // 2]
        line = [picked[base + i * B : base + (i + 1) * B] for i in range(4)]
        low, high, plain = ((line[0], line[2], line[0]), (line[1], line[3], line[3]))[k % 2]
        chosen = jnp.where(side, high, low)
        chosen = jnp.where(along, chosen[half:], chosen[:half])
        dup_ref[pl.ds(k * B, half, stride=2)] = chosen
        dup_ref[pl.ds(k * B + 1, half, stride=2)] = chosen
        coefficient = jnp.where(refined > 0.0, dup_ref[face(k)], plain)
        high, middle, low = (
            held_ref[RIGHT_AT + (4 * i + k) * B : RIGHT_AT + (4 * i + k + 1) * B].astype(F32) for i in range(3)
        )
        right = high + (middle + low)
        faces_ref[face(k)] = right / (4.0 + coefficient) * (1.0 / THETA)


def sweep(field_ref, finish, pieces=1, after=None):
    edge = lax.broadcasted_iota(jnp.int32, (B, LANES), 0)
    is_first, is_last = edge == 0, edge == B - 1

    def plane(index, position):
        start = pl.multiple_of(index * B, B)
        at = pl.ds(start, B)
        centre = field_ref[at]
        if position == 0:
            total = field_ref[pl.ds((index + 1) * B, B)]
            left = pltpu.roll(centre, 1, 0)
        else:
            total = field_ref[pl.ds(pl.multiple_of((index - 1) * B, B), B)]
            left = field_ref[pl.ds(index * B - 1, B)]
        if position == 1:
            total = total + field_ref[pl.ds(pl.multiple_of((index + 1) * B, B), B)]
        if position == 2:
            right = pltpu.roll(centre, B - 1, 0)
        else:
            right = field_ref[pl.ds(index * B + 1, B)]
        total = total + jnp.where(is_first, 0.0, left) + jnp.where(is_last, 0.0, right)
        finish(at, centre, total)

    def step(index, carry):
        plane(index, 1)
        return carry

    plane(0, 0)
    bounds = [max(1, piece * B // pieces) for piece in range(pieces)] + [B - 1]
    for piece in range(pieces):
        lax.fori_loop(bounds[piece], bounds[piece + 1], step, 0, unroll=2)
        if piece == pieces - 1:
            plane(B - 1, 2)
        if after is not None:
            after(piece)


def build_kernel(prev_ref, own_ref, right_in, one_hot_ref, flags_ref, s_ref, inv_ref, diag_ref, part_faces_ref, inv_faces_ref, right_ref, pick_ref, dup_ref, sem):
    read = pltpu.make_async_copy(right_in, right_ref, sem)
    read.start()
    chunk = ROWS // 8
    one_hot = one_hot_ref[...]
    refined, first_bit, second_bit = (flags_ref[i : i + 1] > 0.0 for i in range(3))

    def pick(step, carry):
        at = pl.ds(pl.multiple_of(step * chunk, chunk), chunk)
        both = jnp.concatenate([prev_ref[at], own_ref[at]], axis=1)
        pick_ref[at] = jnp.dot(both, one_hot, preferred_element_type=F32)
        return carry

    lax.fori_loop(0, ROWS // chunk, pick, 0, unroll=2)
    read.wait()
    half = B // 2

    def leaf(row, carry):
        low = pick_ref[pl.ds(pl.multiple_of(row * B, B), B)]
        high = pick_ref[pl.ds(pl.multiple_of((row + half) * B, B), B)]
        chosen = jnp.where(first_bit, high, low)
        chosen = jnp.where(second_bit, chosen[half:], chosen[:half])
        slot = pl.multiple_of((row % 2) * B, B)
        dup_ref[pl.ds(slot, half, stride=2)] = chosen
        dup_ref[pl.ds(slot + 1, half, stride=2)] = chosen
        doubled = dup_ref[pl.ds(slot, B)]
        for k in range(2):
            at = pl.ds(pl.multiple_of((2 * row + k) * B, B), B)
            diag = 4.0 + jnp.where(refined, doubled, pick_ref[at])
            inv = 1.0 / diag
            diag_ref[at] = diag
            inv_ref[at] = inv
            s_ref[at] = right_ref[at] * inv * (1.0 / THETA)
        return carry

    lax.fori_loop(0, half, leaf, 0, unroll=2)

    edge = lax.broadcasted_iota(jnp.int32, (B, LANES), 0)
    inside = (
        s_ref[pl.ds(B, B)],
        s_ref[pl.ds(ROWS - 2 * B, B)],
        s_ref[pl.ds(1, B, stride=B)],
        s_ref[pl.ds(B - 2, B, stride=B)],
    )
    for k, at in enumerate(FACE_SLICES):
        line, inv = s_ref[at], inv_ref[at]
        total = inside[k] + jnp.where(edge == 0, 0.0, pltpu.roll(line, 1, 0))
        total = total + jnp.where(edge == B - 1, 0.0, pltpu.roll(line, B - 1, 0))
        part_faces_ref[face(k)] = SECOND * line + K_1 * (inv * total)
        inv_faces_ref[face(k)] = inv


def gathered(scalar_ref, index, side, source_refs):
    offset = lax.shift_right_logical(index, 7) - scalar_ref[0]
    lane = jnp.broadcast_to(index & (LANES - 1), (B, LANES))
    value = jnp.zeros((B, LANES), F32)
    for number, ref in enumerate(source_refs):
        taken = jnp.take_along_axis(ref[face(side ^ 1)], lane, axis=1, mode="promise_in_bounds")
        value = jnp.where(offset == scalar_ref[1 + number], taken, value)
    return value


def fill_ghost(side, scalar_ref, source_refs, first_ref, second_ref, kind_ref, ghost_ref, pair_ref):
    half = B // 2
    kind = kind_ref[side : side + 1]
    leading, second = (
        gathered(scalar_ref, index_ref[side : side + 1], side, source_refs)
        for index_ref in (first_ref, second_ref)
    )
    at = side * 4 * B
    pair_ref[at : at + B] = leading
    pair_ref[at + B : at + 2 * B] = second
    mean_low = (pair_ref[pl.ds(at, half, stride=2)] + pair_ref[pl.ds(at + 1, half, stride=2)]) * 0.5
    mean_high = (
        pair_ref[pl.ds(at + B, half, stride=2)] + pair_ref[pl.ds(at + B + 1, half, stride=2)]
    ) * 0.5
    for part in range(2):
        for odd in range(2):
            pair_ref[pl.ds(at + (2 + part) * B + odd, half, stride=2)] = leading[
                part * half : (part + 1) * half
            ]
    ghost = jnp.where(kind == 4, jnp.concatenate([mean_low, mean_high], axis=0), 0.0)
    ghost = jnp.where(kind == 1, leading, ghost)
    ghost = jnp.where(kind == 2, pair_ref[at + 2 * B : at + 3 * B], ghost)
    ghost = jnp.where(kind == 3, pair_ref[at + 3 * B : at + 4 * B], ghost)
    ghost_ref[face(side)] = ghost


CORNERS = (
    ((0, 0), (2, 0)),
    ((0, B - 1), (3, 0)),
    ((1, 0), (2, B - 1)),
    ((1, B - 1), (3, B - 1)),
)


def step_faces_kernel(scale, scalar_ref, *refs):
    sources, plan, (part_ref, inv_ref, out_ref, ghost_ref, sum_ref, pair_ref) = refs[:5], refs[5:8], refs[8:]
    for side in range(4):
        fill_ghost(side, scalar_ref, sources, *plan, ghost_ref, pair_ref)
    sum_ref[...] = ghost_ref[...]
    for one, two in CORNERS:
        for (at_face, at_row), (of_face, of_row) in ((one, two), (two, one)):
            at, of = at_face * B + at_row, of_face * B + of_row
            sum_ref[at : at + 1] = sum_ref[at : at + 1] + ghost_ref[of : of + 1]
    out_ref[...] = part_ref[...] + scale * (inv_ref[...] * sum_ref[...])


def step_block_kernel(faces_ref, u_ref, inv_ref, part_ref, part_faces_ref, v_ref):
    def second(at, centre, total):
        v_ref[at] = SECOND * centre + K_1 * (inv_ref[at] * total)

    sweep(u_ref, second)
    for k, at in enumerate(FACE_SLICES):
        v_ref[at] = faces_ref[face(k)]

    def finish(at, centre, total):
        part_ref[at] = (
            (1.0 + C_2 - K_2) * centre + (K_2 * THETA - C_2) * u_ref[at] + K_2 * (inv_ref[at] * total)
        )

    sweep(v_ref, finish)
    for k, at in enumerate(FACE_SLICES):
        part_faces_ref[face(k)] = part_ref[at]


def last_block_kernel(faces_ref, old_ref, right_ref, diag_ref, v_ref, out_ref, residual_ref, edge_ref, part_ref, sems):
    for k, at in enumerate(FACE_SLICES):
        v_ref[at] = faces_ref[face(k)]
    writes = [pltpu.make_async_copy(v_ref, out_ref, sems.at[0])]
    writes[0].start()

    def finish(at, centre, total):
        part_ref[at] = right_ref[at] - diag_ref[at] * centre + total

    def write(quarter):
        at = pl.ds(quarter * (ROWS // 4), ROWS // 4)
        writes.append(pltpu.make_async_copy(part_ref.at[at], residual_ref.at[at], sems.at[1 + quarter]))
        writes[-1].start()

    sweep(v_ref, finish, 4, write)
    edge_ref[0:B] = part_ref[0:B]
    edge_ref[B : 2 * B] = part_ref[ROWS - B : ROWS]
    for plane in range(B):
        for k, tile in enumerate((0, B - 8)):
            to = 2 * B + k * 8 * B + plane * 8
            edge_ref[to : to + 8] = part_ref[plane * B + tile : plane * B + tile + 8]
    for copy in writes:
        copy.wait()


def last_faces_kernel(scalar_ref, *refs):
    sources, plan, refs = (refs[0], *refs[2:5], refs[1]), refs[5:8], refs[8:]
    edge_ref, _, out_ref, ghost_ref, pair_ref, sum_ref, sems = refs
    copies = []
    cells = out_ref.reshape(B, B, LANES)
    for k in range(2):
        tiles = 2 * B + k * 8 * B
        sum_ref[tiles : tiles + 8 * B] = edge_ref[tiles : tiles + 8 * B]
        fill_ghost(2 + k, scalar_ref, sources, *plan, ghost_ref, pair_ref)
        at = pl.ds(tiles + 7 * k, B, stride=8)
        sum_ref[at] = sum_ref[at] + ghost_ref[face(2 + k)]
        of = sum_ref.at[pl.ds(tiles + 8, 8 * (B - 2))].reshape(B - 2, 8, LANES)
        to = cells.at[pl.ds(1, B - 2), pl.ds(k * (B - 8), 8)]
        copies.append(pltpu.make_async_copy(of, to, sems.at[2 + k]))
        copies[-1].start()
    for k in range(2):
        fill_ghost(k, scalar_ref, sources, *plan, ghost_ref, pair_ref)
        sum_ref[face(k)] = edge_ref[face(k)] + ghost_ref[face(k)]
        for (at_face, at_row), (of_face, of_row) in CORNERS[2 * k : 2 * k + 2]:
            at, of = at_face * B + at_row, of_face * B + of_row
            sum_ref[at : at + 1] = sum_ref[at : at + 1] + ghost_ref[of : of + 1]
        to = out_ref.at[pl.ds(k * (ROWS - B), B)]
        copies.append(pltpu.make_async_copy(sum_ref.at[face(k)], to, sems.at[k]))
        copies[-1].start()
    for copy in copies:
        copy.wait()


def swap(value, axis, parity):
    count = lax.axis_size(axis)
    pairs = []
    for low in range(parity, count - 1, 2):
        pairs += [(low, low + 1), (low + 1, low)]
    return lax.ppermute(value, axis, pairs)


def exchange(faces):
    received = [swap(faces, "grp", 1), swap(faces, "sfc", 1), swap(faces, "grp", 0), swap(faces, "sfc", 0)]
    return [(array, VMEM) for array in (faces, *received)]


def body(old_coef, refine_flags, counts, right_side, nbr_first, nbr_second, face_kind):
    grp, sfc = lax.axis_index("grp"), lax.axis_index("sfc")
    n_sfc = lax.axis_size("sfc")
    devices = lax.axis_size(AXES)
    position = grp * n_sfc + sfc
    right = right_side.reshape(ROWS, LANES)
    own = old_coef.reshape(ROWS, LANES)
    prev = lax.ppermute(own, AXES, [(i, i + 1) for i in range(devices - 1)])
    (spread,) = call(
        weights_kernel,
        [(counts, SMEM), (refine_flags.reshape(1, LANES), VMEM)],
        [(kept(devices, jnp.int32), VMEM)],
    )
    weights = lax.all_to_all(spread, AXES, 0, 0, tiled=True)
    even_sfc, even_grp = 1 - 2 * (sfc % 2), n_sfc * (1 - 2 * (grp % 2))
    scalars = jnp.stack([position, 0, -even_grp, -even_sfc, even_grp, even_sfc]).astype(jnp.int32)

    prev, held = call(
        stage_kernel,
        [(prev, ANY), (own, HBM), (right_side, HBM)],
        [(kept(ROWS, jnp.bfloat16), VMEM), (kept(HELD, jnp.bfloat16), VMEM)],
        [vmem(ROWS), pltpu.VMEM((2, B, 8, LANES), F32), vmem(4 * B), pltpu.SemaphoreType.DMA((6,))],
        flops=8_000_000,
    )
    faces, one_hot, flags = call(
        face_kernel,
        [(scalars, SMEM), (weights, VMEM), (held, VMEM)],
        [(kept(4 * B), VMEM), (kept(2 * LANES, jnp.bfloat16), VMEM), (kept(8), VMEM)],
        [vmem(4 * B)],
    )
    neighbours = exchange(faces)
    s1, inv, diag, part_faces, inv_faces, right = call(
        build_kernel,
        [(prev, VMEM), (held, VMEM), (right, HBM), (one_hot, VMEM), (flags, VMEM)],
        [(kept(ROWS), VMEM)] * 3 + [(kept(4 * B), VMEM)] * 2 + [(kept(ROWS), VMEM)],
        [vmem(ROWS), vmem(2 * B), pltpu.SemaphoreType.DMA],
        flops=8_000_000,
    )
    plan = [(nbr_first, VMEM), (nbr_second, VMEM), (face_kind, VMEM)]
    ghost_scratch = [vmem(4 * B), vmem(4 * B), vmem(16 * B)]
    (faces,) = call(
        functools.partial(step_faces_kernel, K_1),
        [(scalars, SMEM), *neighbours, *plan, (part_faces, VMEM), (inv_faces, VMEM)],
        [(kept(4 * B), VMEM)],
        ghost_scratch,
    )
    neighbours = exchange(faces)
    part, part_faces = call(
        step_block_kernel,
        [(faces, VMEM), (s1, VMEM), (inv, VMEM)],
        [(kept(ROWS), VMEM), (kept(4 * B), VMEM)],
        [vmem(ROWS)],
        flops=8_000_000,
    )
    (faces,) = call(
        functools.partial(step_faces_kernel, K_2),
        [(scalars, SMEM), *neighbours, *plan, (part_faces, VMEM), (inv_faces, VMEM)],
        [(kept(4 * B), VMEM)],
        ghost_scratch,
    )
    neighbours = exchange(faces)
    neighbours = [neighbours[0], neighbours[4], *neighbours[1:4]]
    whole = (in_hbm((ROWS, LANES)), HBM)
    _, iterate, residual, edges = call(
        last_block_kernel,
        [(faces, VMEM), (part, VMEM), (right, VMEM), (diag, VMEM)],
        [(kept(ROWS), VMEM), whole, whole, (kept(18 * B), VMEM)],
        [vmem(ROWS), pltpu.SemaphoreType.DMA((5,))],
        aliases={1: 0},
        flops=8_000_000,
    )
    (residual,) = call(
        last_faces_kernel,
        [(scalars, SMEM), *neighbours, *plan, (edges, VMEM), (residual, HBM)],
        [whole],
        [vmem(4 * B), vmem(16 * B), vmem(18 * B), pltpu.SemaphoreType.DMA((4,))],
        aliases={10: 0},
    )
    return iterate.reshape(B, B, LANES), residual.reshape(B, B, LANES)


def solution(mesh):
    leaves, lines = P(None, None, AXES), P(None, AXES)
    return jax.shard_map(
        body,
        mesh=mesh,
        in_specs=(leaves, P(AXES), P(AXES), leaves, lines, lines, lines),
        out_specs=(leaves, leaves),
        check_vma=False,
    )
```
